32 devices in a mesh: groups: 2 (over x), lon: 16 (over z, y, core).
Axes of the slice: x: 2, y: 2, z: 4, core: 2. Of those that a mesh axis runs over, the one named last changes fastest.
Arguments:
- mesh_latent: bfloat16 [3072, 512], P(('groups', 'lon')), parts along dimension 0, may hold values from -6 to 6
- mesh_edges: bfloat16 [36864, 512], P(('groups', 'lon')), parts along dimension 0, may hold values from -6 to 6
- proc_slot: int32 [36864], P(('groups', 'lon')), parts along dimension 0, may hold values from 0 to 127, as said below
- proc_receiver: int32 [36864], P(('groups', 'lon')), parts along dimension 0, may hold values from 0 to 96, as said below
- proc_lists: int32 [512, 8], P(('groups', 'lon')), parts along dimension 0, may hold values from 0 to 95
- grid_latent: bfloat16 [16384, 512], P(('groups', 'lon')), parts along dimension 0, may hold values from -6 to 6
- grid_edges: bfloat16 [49152, 512], P(('groups', 'lon')), parts along dimension 0, may hold values from -6 to 6
- grid_sender: int32 [49152], P(('groups', 'lon')), parts along dimension 0, may hold values from 0 to 1535, as said below
- proc_edge_in: bfloat16 [1536, 512], replicated, may hold values from -0.15625 to 0.15625
- proc_edge_out: bfloat16 [512, 512], replicated, may hold values from -0.25 to 0.25
- proc_node_in: bfloat16 [1024, 512], replicated, may hold values from -0.1875 to 0.1875
- proc_node_out: bfloat16 [512, 512], replicated, may hold values from -0.25 to 0.25
- grid_edge_in: bfloat16 [1536, 512], replicated, may hold values from -0.15625 to 0.15625
- grid_edge_out: bfloat16 [512, 512], replicated, may hold values from -0.25 to 0.25
- grid_node_in: bfloat16 [1024, 512], replicated, may hold values from -0.1875 to 0.1875
- grid_node_out: bfloat16 [512, 512], replicated, may hold values from -0.25 to 0.25
- proc_edge_gain: float32 [512], replicated, may hold values from 0.25 to 1.75
- proc_node_gain: float32 [512], replicated, may hold values from 0.25 to 1.75
- grid_edge_gain: float32 [512], replicated, may hold values from 0.25 to 1.75
- grid_node_gain: float32 [512], replicated, may hold values from 0.25 to 1.75
Outputs:
- mesh_new: bfloat16 [3072, 512], P(('groups', 'lon')), parts along dimension 0
- grid_new: bfloat16 [16384, 512], P(('groups', 'lon')), parts along dimension 0
The draws below stay inside these ranges and needn't reach their ends.
There are 2 independent parts, one for each index of `groups`. The reference program is written for one: setup_inputs(seed, part) draws one part's arguments, and reference() takes and returns one part's arrays. A program takes and returns all parts, laid end to end along the dimension named above; an argument that names none is the same for every part. Nothing has to cross between parts.
Inputs may be any that keep to these rules, and one draw needn't show every extreme that they name: `proc_lists`: every list holds exactly 8 entries; entries may repeat. `proc_slot`: slot s of an edge of device r names column s % 8 of device r's list for owner s // 8. `proc_receiver`: 96 marks an empty slot; on some device no slot is empty. `grid_sender`: the sender of a decoder edge into a grid node of device r is a mesh node of device r - 1, r or r + 1 (modulo 16).
All inputs are finite; a program needn't handle non-finite values.
Results may differ from the reference program's by a relative error of at most 0.011.
Values may be sent and summed in bfloat16 or wider, within the bound.
A program may use at most 128 MiB of HBM per device.

```python
import jax
import jax.numpy as jnp
from jax import lax

D = 512
M_DEV = 96
G_DEV = 512
CAP = 8
NEAR = 3
E_DEV = 1152
MESH = 1536
MESH_EDGES = 18432
GRID = 8192
GRID_EDGES = 24576
N_LON = 16


def draw_proc_slot(key, part):
    key = jax.random.fold_in(key, 11)
    near_key, shift_key, far_key, col_key = jax.random.split(key, 4)
    total = E_DEV * N_LON
    device = jnp.arange(total, dtype=jnp.int32) // E_DEV
    nearby = jax.random.randint(near_key, (total,), 0, 10) < 7
    offsets = jax.random.randint(shift_key, (total,), -2, 3)
    distant = jax.random.randint(far_key, (total,), 0, N_LON)
    owner_dev = jnp.where(nearby, (device + offsets) % N_LON, distant)
    columns = jax.random.randint(col_key, (total,), 0, CAP)
    slots = owner_dev * CAP + columns
    slots = slots.at[0].set(0)
    slots = slots.at[total - 1].set(N_LON * CAP - 1)
    return slots.astype(jnp.int32)


def draw_proc_receiver(key, part):
    key = jax.random.fold_in(key, 12)
    live_key, full_key, perm_key, row_key = jax.random.split(key, 4)
    lowest = 2 * E_DEV // 5
    live = jax.random.randint(live_key, (N_LON,), lowest, E_DEV + 1)
    full_dev = jax.random.randint(full_key, (), 0, N_LON)
    live = live.at[(full_dev + N_LON // 2) % N_LON].set(lowest)
    live = live.at[full_dev].set(E_DEV)
    ranks = jax.vmap(lambda each: jax.random.permutation(each, E_DEV))(jax.random.split(perm_key, N_LON))
    targets = jax.random.randint(row_key, (N_LON, E_DEV), 0, M_DEV)
    chosen = jnp.where(ranks < live[:, None], targets, M_DEV)
    return chosen.reshape(-1).astype(jnp.int32)


def draw_grid_sender(key, part):
    key = jax.random.fold_in(key, 13)
    shift_key, row_key = jax.random.split(key, 2)
    total = NEAR * G_DEV * N_LON
    device = jnp.arange(total, dtype=jnp.int32) // (NEAR * G_DEV)
    offsets = jax.random.randint(shift_key, (total,), -1, 2)
    offsets = offsets.at[0].set(0).at[total - 1].set(0)
    rows = jax.random.randint(row_key, (total,), 0, M_DEV)
    rows = rows.at[0].set(0).at[total - 1].set(M_DEV - 1)
    owner_dev = (device + offsets) % N_LON
    return (owner_dev * M_DEV + rows).astype(jnp.int32)


def plant(values, own_key, least, high):
    shape = values.shape
    index_at = [jax.random.randint(jax.random.fold_in(own_key, axis), (), 0, shape[axis]) for axis in range(len(shape))]
    values = values.at[tuple(index_at)].set(least)
    longest = shape.index(max(shape))
    index_at[longest] = (index_at[longest] + 1) % shape[longest]
    return values.at[tuple(index_at)].set(high)


def shard_levels(rng, extent, cuts, least, high):
    level = 1.0
    for position, shards_of in cuts:
        steps = jax.random.uniform(jax.random.fold_in(jax.random.fold_in(rng, 6), position), (shards_of,), jnp.float32, least / len(cuts), high / len(cuts))
        level = level * jnp.repeat(jnp.exp(steps), extent[position] // shards_of).reshape((-1,) + (1,) * (len(extent) - 1 - position))
    return level


def centred(stream_key, dims, scale, most, shards=(), kind=jnp.bfloat16):
    loudness = shard_levels(stream_key, dims, shards, -0.22, 0.18) if shards else 1.0
    values = jax.random.normal(stream_key, dims, jnp.float32) * scale * loudness
    return jnp.minimum(jnp.maximum(values, -most), most).astype(kind)


def setup_inputs(seed: int = 0, part: int = 0) -> dict:
    streams_of = jax.random.split(jax.random.key(seed), 21)
    part_keys = jax.random.split(jax.random.fold_in(streams_of[20], part), 21)
    return {
        "mesh_latent": centred(part_keys[0], (MESH, D), 1.0, 6.0, ((0, 16),)),
        "mesh_edges": centred(part_keys[1], (MESH_EDGES, D), 1.0, 6.0, ((0, 16),)),
        "proc_slot": draw_proc_slot(jax.random.fold_in(jax.random.fold_in(streams_of[20], part), 71), part),
        "proc_receiver": draw_proc_receiver(jax.random.fold_in(jax.random.fold_in(streams_of[20], part), 71), part),
        "proc_lists": plant(jax.random.randint(part_keys[4], (N_LON * N_LON, CAP), 0, M_DEV), jax.random.fold_in(part_keys[4], 1), 0, M_DEV - 1).astype(jnp.int32),
        "grid_latent": centred(part_keys[5], (GRID, D), 1.0, 6.0, ((0, 16),)),
        "grid_edges": centred(part_keys[6], (GRID_EDGES, D), 1.0, 6.0, ((0, 16),)),
        "grid_sender": draw_grid_sender(jax.random.fold_in(jax.random.fold_in(streams_of[20], part), 71), part),
        "proc_edge_in": centred(streams_of[8], (3 * D, D), (3 * D) ** -0.5, 0.15625),
        "proc_edge_out": centred(streams_of[9], (D, D), D ** -0.5, 0.25),
        "proc_node_in": centred(streams_of[10], (2 * D, D), (2 * D) ** -0.5, 0.1875),
        "proc_node_out": centred(streams_of[11], (D, D), D ** -0.5, 0.25),
        "grid_edge_in": centred(streams_of[12], (3 * D, D), (3 * D) ** -0.5, 0.15625),
        "grid_edge_out": centred(streams_of[13], (D, D), D ** -0.5, 0.25),
        "grid_node_in": centred(streams_of[14], (2 * D, D), (2 * D) ** -0.5, 0.1875),
        "grid_node_out": centred(streams_of[15], (D, D), D ** -0.5, 0.25),
        "proc_edge_gain": jnp.clip(1.0 + 0.15 * jax.random.normal(streams_of[16], (D,), jnp.float32), 0.25, 1.75),
        "proc_node_gain": jnp.clip(1.0 + 0.15 * jax.random.normal(streams_of[17], (D,), jnp.float32), 0.25, 1.75),
        "grid_edge_gain": jnp.clip(1.0 + 0.15 * jax.random.normal(streams_of[18], (D,), jnp.float32), 0.25, 1.75),
        "grid_node_gain": jnp.clip(1.0 + 0.15 * jax.random.normal(streams_of[19], (D,), jnp.float32), 0.25, 1.75),
    }


EPSILON = 1e-05

def layer_norm(values, gain):
    center = values - lax.optimization_barrier(jnp.mean(values, axis=-1, keepdims=True))
    spread = lax.optimization_barrier(jnp.mean(center * center, axis=-1, keepdims=True))
    return center * lax.rsqrt(spread + EPSILON) * gain

def two_layer(inputs, w_first, w_second, gain):
    hidden = jax.nn.silu(jnp.dot(inputs, w_first, preferred_element_type=jnp.float32)).astype(jnp.bfloat16)
    return layer_norm(jnp.dot(hidden, w_second, preferred_element_type=jnp.float32), gain)

def reference(mesh_latent, mesh_edges, proc_slot, proc_receiver, proc_lists, grid_latent, grid_edges, grid_sender, proc_edge_in, proc_edge_out, proc_node_in, proc_node_out, grid_edge_in, grid_edge_out, grid_node_in, grid_node_out, proc_edge_gain, proc_node_gain, grid_edge_gain, grid_node_gain):
    device = jnp.arange(E_DEV * N_LON, dtype=jnp.int32) // E_DEV
    owner_dev = (proc_slot // CAP).astype(jnp.int32)
    list_col = (proc_slot % CAP).astype(jnp.int32)
    local_row = proc_lists[device * N_LON + owner_dev, list_col]
    sender_id = owner_dev * M_DEV + local_row
    receiver_id = device * M_DEV + jnp.minimum(proc_receiver, M_DEV - 1)

    def proc_block(pieces):
        edge_blk, send_blk, recv_blk, recv_local = pieces
        inputs = jnp.concatenate([edge_blk, mesh_latent[send_blk], mesh_latent[recv_blk]], axis=1)
        message = two_layer(inputs, proc_edge_in, proc_edge_out, proc_edge_gain).astype(jnp.bfloat16)
        one_hot = (jnp.arange(M_DEV, dtype=jnp.int32)[:, None] == recv_local[None, :]).astype(jnp.bfloat16)
        return jnp.dot(one_hot, message, preferred_element_type=jnp.float32)
    incoming = lax.map(proc_block, (mesh_edges.reshape(N_LON, E_DEV, D), sender_id.reshape(N_LON, E_DEV), receiver_id.reshape(N_LON, E_DEV), proc_receiver.reshape(N_LON, E_DEV)))
    incoming = incoming.reshape(M_DEV * N_LON, D).astype(jnp.bfloat16)
    node_inputs = jnp.concatenate([mesh_latent, incoming], axis=1)
    mesh_new = (mesh_latent.astype(jnp.float32) + two_layer(node_inputs, proc_node_in, proc_node_out, proc_node_gain)).astype(jnp.bfloat16)

    def grid_block(pieces):
        edge_blk, send_blk, node_blk = pieces
        receivers = jnp.repeat(node_blk, NEAR, axis=0)
        inputs = jnp.concatenate([edge_blk, mesh_new[send_blk], receivers], axis=1)
        message = two_layer(inputs, grid_edge_in, grid_edge_out, grid_edge_gain).astype(jnp.bfloat16)
        return lax.optimization_barrier(jnp.sum(message.astype(jnp.float32).reshape(G_DEV, NEAR, D), axis=1))
    grid_incoming = lax.map(grid_block, (grid_edges.reshape(N_LON, NEAR * G_DEV, D), grid_sender.reshape(N_LON, NEAR * G_DEV), grid_latent.reshape(N_LON, G_DEV, D)))
    grid_incoming = grid_incoming.reshape(G_DEV * N_LON, D).astype(jnp.bfloat16)
    grid_inputs = jnp.concatenate([grid_latent, grid_incoming], axis=1)
    grid_new = (grid_latent.astype(jnp.float32) + two_layer(grid_inputs, grid_node_in, grid_node_out, grid_node_gain)).astype(jnp.bfloat16)
    return (mesh_new, grid_new)
```

```python
import functools

import jax
import jax.numpy as jnp
from jax import lax
from jax.experimental import pallas as pl
from jax.experimental.pallas import tpu as pltpu
from jax.sharding import PartitionSpec as P

NEAR = 3
EPSILON = 1e-05
BLOCK = 384
LANES = 128
BF16 = jnp.bfloat16
F32 = jnp.float32
MESH_ID = pl.DeviceIdType.MESH


def mm(a, b):
    return jnp.dot(a, b, preferred_element_type=F32)


def mm_t(a, b):
    return lax.dot_general(a, b, (((0,), (0,)), ((), ())), preferred_element_type=F32)


def pick(flags):
    return jnp.where(flags, 1.0, 0.0).astype(BF16)


def act(first_sum):
    half = 0.5 * first_sum
    return (half + half * jnp.tanh(half)).astype(BF16)


def norm(values, gain):
    center = values - jnp.mean(values, axis=-1, keepdims=True)
    spread = jnp.mean(center * center, axis=-1, keepdims=True)
    return center * lax.rsqrt(spread + EPSILON) * gain


def iota(shape, dim):
    return lax.broadcasted_iota(jnp.int32, shape, dim)


def kernel(
    n,
    lat,
    slot,
    recv,
    lists,
    gsend,
    pe_gain,
    pn_gain,
    ge_gain,
    gn_gain,
    *refs,
):
    hbm = refs[:11]
    mesh_out, grid_out = refs[11:13]
    vm = refs[13:24]
    (
        list_src,
        list_dst,
        rows_src,
        rows_dst,
        term_pad,
        table,
        edge_acc,
        grid_acc,
        gnode_acc,
        incoming,
        own_term,
        side_term,
        gin,
        load_sem,
        list_send,
        list_recv,
        rows_send,
        rows_recv,
        side_send,
        side_recv,
    ) = refs[24:]
    edges, glat, gedges, pe_in, pe_out, pn_in, pn_out, ge_in, ge_out, gn_in, gn_out = vm
    order = (3, 0, 5, 7, 2, 1, 9, 4, 6, 8, 10)

    def load(k):
        return pltpu.make_async_copy(hbm[k], vm[k], load_sem.at[k])

    for k in order:
        load(k).start()

    me = lax.axis_index("lon")
    rows, width = lat.shape
    cap = lists.shape[1]
    half = width // 2
    n_tab = n * cap
    n_edges = edges.shape[0]
    n_gedges = gedges.shape[0]
    n_grid = glat.shape[0]
    nodes = BLOCK // NEAR

    def at(distance):
        return lax.rem(me + distance + n, n)

    barrier = pltpu.get_barrier_semaphore()

    def greet(d, carry):
        pl.semaphore_signal(barrier, inc=1, device_id={"lon": at(d)}, device_id_type=MESH_ID)
        return carry

    lax.fori_loop(1, n, greet, 0)

    def spread_list(o, carry):
        row = jnp.broadcast_to(lists[pl.ds(o, 1), :].astype(F32), (cap, cap))
        kept = jnp.where(iota((cap, cap), 0) == iota((cap, cap), 1), row, 0.0)
        column = jnp.sum(kept, axis=1, keepdims=True)
        list_src[o] = jnp.broadcast_to(column, (cap, LANES)).astype(jnp.int32)
        return carry

    lax.fori_loop(0, n, spread_list, 0)
    pl.semaphore_wait(barrier, n - 1)

    def list_copy(d):
        return pltpu.make_async_remote_copy(
            src_ref=list_src.at[at(d)],
            dst_ref=list_dst.at[d],
            send_sem=list_send,
            recv_sem=list_recv,
            device_id={"lon": at(d)},
            device_id_type=MESH_ID,
        )

    def send_list(d, carry):
        list_copy(d).start()
        return carry

    lax.fori_loop(1, n, send_list, 0)
    list_dst[0] = list_src[me]

    load(3).wait()
    lat_v = lat[...]
    term_pad[...] = jnp.zeros_like(term_pad)
    term_pad[0:rows, :] = mm(lat_v, pe_in[width : 2 * width, :]).astype(BF16)
    table[n_tab:, :] = jnp.zeros((LANES, width), BF16)
    table[n_tab : n_tab + rows, :] = mm(lat_v, pe_in[2 * width :, :]).astype(BF16)

    load(0).wait()

    def edge_first(b, carry):
        here = pl.ds(pl.multiple_of(b * BLOCK, BLOCK), BLOCK)
        edge_acc[here, :] = mm(edges[here, :], pe_in[0:width, :])
        return carry

    lax.fori_loop(0, n_edges // BLOCK, edge_first, 0)

    got = list_dst.at[pl.ds(1, n - 1)]
    pltpu.make_async_copy(got, got, list_recv).wait()
    wanted = list_dst[...].reshape(n_tab, LANES)
    chosen = pick(wanted == iota((n_tab, LANES), 1))
    left_half = mm(chosen, term_pad[:, 0:half]).reshape(n, cap, half)
    right_half = mm(chosen, term_pad[:, half:]).reshape(n, cap, half)
    rows_src[...] = (
        jnp.concatenate([left_half, right_half], axis=1).reshape(n_tab * 2, half).astype(BF16)
    )
    chunk = 2 * cap

    def rows_copy(d):
        return pltpu.make_async_remote_copy(
            src_ref=rows_src.at[pl.ds(pl.multiple_of(d * chunk, chunk), chunk), :],
            dst_ref=rows_dst.at[pl.ds(pl.multiple_of((n - d) * chunk, chunk), chunk), :],
            send_sem=rows_send,
            recv_sem=rows_recv,
            device_id={"lon": at(-d)},
            device_id_type=MESH_ID,
        )

    def send_rows(d, carry):
        rows_copy(d).start()
        return carry

    lax.fori_loop(1, n, send_rows, 0)
    rows_dst[0:chunk, :] = rows_src[0:chunk, :]

    load(5).wait()
    load(7).wait()
    load(2).wait()
    load(1).wait()
    node_own = mm(lat_v, pn_in[0:width, :])
    repeat = pick(iota((BLOCK, nodes), 0) // NEAR == iota((BLOCK, nodes), 1))

    def grid_first(b, carry):
        here = pl.ds(pl.multiple_of(b * BLOCK, BLOCK), BLOCK)
        there = pl.ds(pl.multiple_of(b * nodes, nodes), nodes)
        term = mm(glat[there, :], ge_in[2 * width :, :]).astype(BF16)
        grid_acc[here, :] = mm(gedges[here, :], ge_in[0:width, :]) + mm(repeat, term)
        return carry

    lax.fori_loop(0, n_gedges // BLOCK, grid_first, 0)
    load(9).wait()
    gnode_acc[...] = mm(glat[...], gn_in[0:width, :])
    load(4).wait()
    load(6).wait()

    arrived = rows_dst.at[pl.ds(chunk, (n - 1) * chunk), :]
    pltpu.make_async_copy(arrived, arrived, rows_recv).wait()
    parts = rows_dst[...].astype(F32).reshape(n, 2, cap, half)
    table[0:n_tab, :] = jnp.concatenate(
        [parts[:, 0].reshape(n_tab, half), parts[:, 1].reshape(n_tab, half)], axis=1
    ).astype(BF16)

    distance = me - iota((n, cap, BLOCK), 0)
    owner = jnp.where(distance < 0, distance + n, distance)
    slot_of = (owner * cap + iota((n, cap, BLOCK), 1)).reshape(n_tab, BLOCK)
    incoming[...] = jnp.zeros_like(incoming)

    def edge_second(b, carry):
        here = pl.ds(pl.multiple_of(b * BLOCK, BLOCK), BLOCK)
        slots = slot[:, here]
        receivers = recv[:, here]
        gather = jnp.concatenate(
            [
                pick(slot_of == slots),
                pick(iota((LANES, BLOCK), 0) == jnp.minimum(receivers, rows - 1)),
            ],
            axis=0,
        )
        total = edge_acc[here, :] + mm_t(gather, table[...])
        message = norm(mm(act(total), pe_out[...]), pe_gain[...]).astype(BF16)
        incoming[...] += mm(pick(iota((rows, BLOCK), 0) == receivers), message)
        return carry

    lax.fori_loop(0, n_edges // BLOCK, edge_second, 0)

    node_sum = node_own + mm(incoming[...].astype(BF16), pn_in[width:, :])
    mesh_new = (
        lat_v.astype(F32) + norm(mm(act(node_sum), pn_out[...]), pn_gain[...])
    ).astype(BF16)
    mesh_out[...] = mesh_new
    own_term[...] = mm(mesh_new, ge_in[width : 2 * width, :]).astype(BF16)

    def side_copy(side):
        return pltpu.make_async_remote_copy(
            src_ref=own_term,
            dst_ref=side_term.at[pl.ds(side * rows, rows), :],
            send_sem=side_send.at[side],
            recv_sem=side_recv.at[side],
            device_id={"lon": at(1 - 2 * side)},
            device_id_type=MESH_ID,
        )

    side_copy(0).start()
    side_copy(1).start()
    load(8).wait()
    load(10).wait()

    def grid_own(b, carry):
        here = pl.ds(pl.multiple_of(b * BLOCK, BLOCK), BLOCK)
        gather = pick(iota((rows, BLOCK), 0) + me * rows == gsend[:, here])
        grid_acc[here, :] += mm_t(gather, own_term[...])
        return carry

    lax.fori_loop(0, n_gedges // BLOCK, grid_own, 0)
    side_copy(0).wait_recv()
    side_copy(1).wait_recv()
    pooled = pick(iota((nodes, BLOCK), 1) // NEAR == iota((nodes, BLOCK), 0))
    side_index = jnp.concatenate(
        [iota((rows, BLOCK), 0) + at(-1) * rows, iota((rows, BLOCK), 0) + at(1) * rows], axis=0
    )

    def grid_second(b, carry):
        here = pl.ds(pl.multiple_of(b * BLOCK, BLOCK), BLOCK)
        there = pl.ds(pl.multiple_of(b * nodes, nodes), nodes)
        gather = pick(side_index == gsend[:, here])
        total = grid_acc[here, :] + mm_t(gather, side_term[...])
        message = norm(mm(act(total), ge_out[...]), ge_gain[...]).astype(BF16)
        gin[there, :] = mm(pooled, message).astype(BF16)
        return carry

    lax.fori_loop(0, n_gedges // BLOCK, grid_second, 0)

    def grid_node(b, carry):
        there = pl.ds(pl.multiple_of(b * (n_grid // 2), n_grid // 2), n_grid // 2)
        total = gnode_acc[there, :] + mm(gin[there, :], gn_in[width:, :])
        update = norm(mm(act(total), gn_out[...]), gn_gain[...])
        grid_out[there, :] = (glat[there, :].astype(F32) + update).astype(BF16)
        return carry

    lax.fori_loop(0, 2, grid_node, 0)

    sent = list_src.at[pl.ds(1, n - 1)]
    pltpu.make_async_copy(sent, sent, list_send).wait()
    gone = rows_src.at[pl.ds(chunk, (n - 1) * chunk), :]
    pltpu.make_async_copy(gone, gone, rows_send).wait()
    side_copy(0).wait_send()
    side_copy(1).wait_send()


def local(
    mesh_latent,
    mesh_edges,
    proc_slot,
    proc_receiver,
    proc_lists,
    grid_latent,
    grid_edges,
    grid_sender,
    proc_edge_in,
    proc_edge_out,
    proc_node_in,
    proc_node_out,
    grid_edge_in,
    grid_edge_out,
    grid_node_in,
    grid_node_out,
    proc_edge_gain,
    proc_node_gain,
    grid_edge_gain,
    grid_node_gain,
):
    n = lax.axis_size("lon")
    rows, width = mesh_latent.shape
    cap = proc_lists.shape[1]
    n_tab = n * cap
    n_edges = mesh_edges.shape[0]
    n_gedges = grid_edges.shape[0]
    n_grid = grid_latent.shape[0]
    big = (
        mesh_edges,
        grid_latent,
        grid_edges,
        proc_edge_in,
        proc_edge_out,
        proc_node_in,
        proc_node_out,
        grid_edge_in,
        grid_edge_out,
        grid_node_in,
        grid_node_out,
    )
    small = (
        mesh_latent,
        proc_slot.reshape(1, -1),
        proc_receiver.reshape(1, -1),
        proc_lists,
        grid_sender.reshape(1, -1),
        proc_edge_gain.reshape(1, -1),
        proc_node_gain.reshape(1, -1),
        grid_edge_gain.reshape(1, -1),
        grid_node_gain.reshape(1, -1),
    )
    vmem = pl.BlockSpec(memory_space=pltpu.VMEM)
    return pl.pallas_call(
        functools.partial(kernel, n),
        out_shape=(
            jax.ShapeDtypeStruct(mesh_latent.shape, BF16),
            jax.ShapeDtypeStruct(grid_latent.shape, BF16),
        ),
        in_specs=[vmem] * len(small) + [pl.BlockSpec(memory_space=pl.ANY)] * len(big),
        out_specs=(vmem, vmem),
        scratch_shapes=[pltpu.VMEM(a.shape, a.dtype) for a in big]
        + [
            pltpu.VMEM((n, cap, LANES), jnp.int32),
            pltpu.VMEM((n, cap, LANES), jnp.int32),
            pltpu.VMEM((n_tab * 2, width // 2), BF16),
            pltpu.VMEM((n_tab * 2, width // 2), BF16),
            pltpu.VMEM((LANES, width), BF16),
            pltpu.VMEM((n_tab + LANES, width), BF16),
            pltpu.VMEM((n_edges, width), F32),
            pltpu.VMEM((n_gedges, width), F32),
            pltpu.VMEM((n_grid, width), F32),
            pltpu.VMEM((rows, width), F32),
            pltpu.VMEM((rows, width), BF16),
            pltpu.VMEM((2 * rows, width), BF16),
            pltpu.VMEM((n_grid, width), BF16),
            pltpu.SemaphoreType.DMA((len(big),)),
            pltpu.SemaphoreType.DMA,
            pltpu.SemaphoreType.DMA,
            pltpu.SemaphoreType.DMA,
            pltpu.SemaphoreType.DMA,
            pltpu.SemaphoreType.DMA((2,)),
            pltpu.SemaphoreType.DMA((2,)),
        ],
        compiler_params=pltpu.CompilerParams(
            collective_id=0, has_side_effects=True, vmem_limit_bytes=50 * 1024 * 1024
        ),
    )(*small, *big)


def solution(mesh):
    rows = P(("groups", "lon"), None)
    flat = P(("groups", "lon"))
    placed = (rows, rows, flat, flat, rows, rows, rows, flat) + (P(),) * 12
    return jax.shard_map(
        local,
        mesh=mesh,
        in_specs=placed,
        out_specs=(rows, rows),
        check_vma=False,
    )
```

```python
import functools

import jax
import jax.numpy as jnp
from jax import lax
from jax.experimental import pallas as pl
from jax.experimental.pallas import tpu as pltpu
from jax.sharding import PartitionSpec as P

NEAR = 3
EPSILON = 1e-05
BLOCK = 384
LANES = 128
BF16 = jnp.bfloat16
F32 = jnp.float32
MESH_ID = pl.DeviceIdType.MESH


def mm(a, b):
    return jnp.dot(a, b, preferred_element_type=F32)


def mm_t(a, b):
    return lax.dot_general(a, b, (((0,), (0,)), ((), ())), preferred_element_type=F32)


def pick(flags):
    return jnp.where(flags, 1.0, 0.0).astype(BF16)


def act(first_sum):
    half = 0.5 * first_sum
    return (half + half * jnp.tanh(half)).astype(BF16)


def norm(values, gain):
    center = values - jnp.mean(values, axis=-1, keepdims=True)
    spread = jnp.mean(center * center, axis=-1, keepdims=True)
    return center * lax.rsqrt(spread + EPSILON) * gain


def iota(shape, dim):
    return lax.broadcasted_iota(jnp.int32, shape, dim)


def kernel(
    n,
    *refs,
):
    hbm = refs[:20]
    mesh_out, grid_out = refs[20:22]
    vm = refs[22:42]
    (
        slot,
        recv,
        gsend,
        list_src,
        list_dst,
        rows_src,
        rows_dst,
        term_pad,
        table,
        edge_acc,
        grid_acc,
        gnode_acc,
        incoming,
        own_term,
        side_term,
        gin,
        load_sem,
        list_send,
        list_recv,
        rows_send,
        rows_recv,
        side_send,
        side_recv,
    ) = refs[42:]
    edges, glat, gedges, pe_in, pe_out, pn_in, pn_out, ge_in, ge_out, gn_in, gn_out = vm[:11]
    lat, lists, slot_flat, recv_flat, gsend_flat, pe_gain, pn_gain, ge_gain, gn_gain = vm[11:]
    order = (12, 11, 3, 0, 13, 14, 5, 7, 2, 1, 9, 4, 6, 15, 16, 17, 18, 19, 8, 10)

    def load(k):
        return pltpu.make_async_copy(hbm[k], vm[k], load_sem.at[k])

    for k in order:
        load(k).start()

    me = lax.axis_index("lon")
    rows, width = lat.shape
    cap = lists.shape[0]
    half = width // 2
    n_tab = n * cap
    n_edges = edges.shape[0]
    n_gedges = gedges.shape[0]
    n_grid = glat.shape[0]
    nodes = BLOCK // NEAR

    def at(distance):
        return lax.rem(me + distance + n, n)

    barrier = pltpu.get_barrier_semaphore()

    def greet(d, carry):
        pl.semaphore_signal(barrier, inc=1, device_id={"lon": at(d)}, device_id_type=MESH_ID)
        return carry

    lax.fori_loop(1, n, greet, 0)

    def spread_list(o, carry):
        kept = jnp.where(iota((cap, n), 1) == o, lists[...].astype(F32), 0.0)
        column = jnp.sum(kept, axis=1, keepdims=True)
        list_src[o] = jnp.broadcast_to(column, (cap, LANES)).astype(jnp.int32)
        return carry

    load(12).wait()
    lax.fori_loop(0, n, spread_list, 0)
    pl.semaphore_wait(barrier, n - 1)

    def list_copy(d):
        return pltpu.make_async_remote_copy(
            src_ref=list_src.at[at(d)],
            dst_ref=list_dst.at[d],
            send_sem=list_send,
            recv_sem=list_recv,
            device_id={"lon": at(d)},
            device_id_type=MESH_ID,
        )

    def send_list(d, carry):
        list_copy(d).start()
        return carry

    lax.fori_loop(1, n, send_list, 0)
    list_dst[0] = list_src[me]

    load(11).wait()
    load(3).wait()
    lat_v = lat[...]
    term_pad[...] = jnp.zeros_like(term_pad)
    term_pad[0:rows, :] = mm(lat_v, pe_in[width : 2 * width, :]).astype(BF16)
    table[n_tab:, :] = jnp.zeros((LANES, width), BF16)
    table[n_tab : n_tab + rows, :] = mm(lat_v, pe_in[2 * width :, :]).astype(BF16)

    load(0).wait()

    def edge_first(b, carry):
        here = pl.ds(pl.multiple_of(b * BLOCK, BLOCK), BLOCK)
        edge_acc[here, :] = mm(edges[here, :], pe_in[0:width, :])
        return carry

    lax.fori_loop(0, n_edges // BLOCK, edge_first, 0)

    got = list_dst.at[pl.ds(1, n - 1)]
    pltpu.make_async_copy(got, got, list_recv).wait()
    wanted = list_dst[...].reshape(n_tab, LANES)
    chosen = pick(wanted == iota((n_tab, LANES), 1))
    left_half = mm(chosen, term_pad[:, 0:half]).reshape(n, cap, half)
    right_half = mm(chosen, term_pad[:, half:]).reshape(n, cap, half)
    rows_src[...] = (
        jnp.concatenate([left_half, right_half], axis=1).reshape(n_tab * 2, half).astype(BF16)
    )
    chunk = 2 * cap

    def rows_copy(d):
        return pltpu.make_async_remote_copy(
            src_ref=rows_src.at[pl.ds(pl.multiple_of(d * chunk, chunk), chunk), :],
            dst_ref=rows_dst.at[pl.ds(pl.multiple_of((n - d) * chunk, chunk), chunk), :],
            send_sem=rows_send,
            recv_sem=rows_recv,
            device_id={"lon": at(-d)},
            device_id_type=MESH_ID,
        )

    def send_rows(d, carry):
        rows_copy(d).start()
        return carry

    lax.fori_loop(1, n, send_rows, 0)
    rows_dst[0:chunk, :] = rows_src[0:chunk, :]

    for k in (13, 14, 5, 7):
        load(k).wait()
    slot[...] = slot_flat[...].reshape(1, n_edges)
    recv[...] = recv_flat[...].reshape(1, n_edges)
    load(2).wait()
    load(1).wait()
    node_own = mm(lat_v, pn_in[0:width, :])
    repeat = pick(iota((BLOCK, nodes), 0) // NEAR == iota((BLOCK, nodes), 1))

    def grid_first(b, carry):
        here = pl.ds(pl.multiple_of(b * BLOCK, BLOCK), BLOCK)
        there = pl.ds(pl.multiple_of(b * nodes, nodes), nodes)
        term = mm(glat[there, :], ge_in[2 * width :, :]).astype(BF16)
        grid_acc[here, :] = mm(gedges[here, :], ge_in[0:width, :]) + mm(repeat, term)
        return carry

    lax.fori_loop(0, n_gedges // BLOCK, grid_first, 0)
    load(9).wait()
    gnode_acc[...] = mm(glat[...], gn_in[0:width, :])
    for k in (4, 6, 15, 16, 17, 18, 19):
        load(k).wait()
    gsend[...] = gsend_flat[...].reshape(1, n_gedges)

    arrived = rows_dst.at[pl.ds(chunk, (n - 1) * chunk), :]
    pltpu.make_async_copy(arrived, arrived, rows_recv).wait()
    parts = rows_dst[...].astype(F32).reshape(n, 2, cap, half)
    table[0:n_tab, :] = jnp.concatenate(
        [parts[:, 0].reshape(n_tab, half), parts[:, 1].reshape(n_tab, half)], axis=1
    ).astype(BF16)

    distance = me - iota((n, cap, BLOCK), 0)
    owner = jnp.where(distance < 0, distance + n, distance)
    slot_of = (owner * cap + iota((n, cap, BLOCK), 1)).reshape(n_tab, BLOCK)
    incoming[...] = jnp.zeros_like(incoming)

    def edge_second(b, carry):
        here = pl.ds(pl.multiple_of(b * BLOCK, BLOCK), BLOCK)
        slots = slot[:, here]
        receivers = recv[:, here]
        gather = jnp.concatenate(
            [
                pick(slot_of == slots),
                pick(iota((LANES, BLOCK), 0) == jnp.minimum(receivers, rows - 1)),
            ],
            axis=0,
        )
        total = edge_acc[here, :] + mm_t(gather, table[...])
        message = norm(mm(act(total), pe_out[...]), pe_gain[...]).astype(BF16)
        incoming[...] += mm(pick(iota((rows, BLOCK), 0) == receivers), message)
        return carry

    lax.fori_loop(0, n_edges // BLOCK, edge_second, 0)

    node_sum = node_own + mm(incoming[...].astype(BF16), pn_in[width:, :])
    mesh_new = (
        lat_v.astype(F32) + norm(mm(act(node_sum), pn_out[...]), pn_gain[...])
    ).astype(BF16)
    mesh_out[...] = mesh_new
    own_term[...] = mm(mesh_new, ge_in[width : 2 * width, :]).astype(BF16)

    def side_copy(side):
        return pltpu.make_async_remote_copy(
            src_ref=own_term,
            dst_ref=side_term.at[pl.ds(side * rows, rows), :],
            send_sem=side_send.at[side],
            recv_sem=side_recv.at[side],
            device_id={"lon": at(1 - 2 * side)},
            device_id_type=MESH_ID,
        )

    side_copy(0).start()
    side_copy(1).start()
    load(8).wait()
    load(10).wait()

    def grid_own(b, carry):
        here = pl.ds(pl.multiple_of(b * BLOCK, BLOCK), BLOCK)
        gather = pick(iota((rows, BLOCK), 0) + me * rows == gsend[:, here])
        grid_acc[here, :] += mm_t(gather, own_term[...])
        return carry

    lax.fori_loop(0, n_gedges // BLOCK, grid_own, 0)
    side_copy(0).wait_recv()
    side_copy(1).wait_recv()
    pooled = pick(iota((nodes, BLOCK), 1) // NEAR == iota((nodes, BLOCK), 0))
    side_index = jnp.concatenate(
        [iota((rows, BLOCK), 0) + at(-1) * rows, iota((rows, BLOCK), 0) + at(1) * rows], axis=0
    )

    def grid_second(b, carry):
        here = pl.ds(pl.multiple_of(b * BLOCK, BLOCK), BLOCK)
        there = pl.ds(pl.multiple_of(b * nodes, nodes), nodes)
        gather = pick(side_index == gsend[:, here])
        total = grid_acc[here, :] + mm_t(gather, side_term[...])
        message = norm(mm(act(total), ge_out[...]), ge_gain[...]).astype(BF16)
        gin[there, :] = mm(pooled, message).astype(BF16)
        return carry

    lax.fori_loop(0, n_gedges // BLOCK, grid_second, 0)

    def grid_node(b, carry):
        there = pl.ds(pl.multiple_of(b * (n_grid // 2), n_grid // 2), n_grid // 2)
        total = gnode_acc[there, :] + mm(gin[there, :], gn_in[width:, :])
        update = norm(mm(act(total), gn_out[...]), gn_gain[...])
        grid_out[there, :] = (glat[there, :].astype(F32) + update).astype(BF16)
        return carry

    lax.fori_loop(0, 2, grid_node, 0)

    sent = list_src.at[pl.ds(1, n - 1)]
    pltpu.make_async_copy(sent, sent, list_send).wait()
    gone = rows_src.at[pl.ds(chunk, (n - 1) * chunk), :]
    pltpu.make_async_copy(gone, gone, rows_send).wait()
    side_copy(0).wait_send()
    side_copy(1).wait_send()


def local(
    mesh_latent,
    mesh_edges,
    proc_slot,
    proc_receiver,
    proc_lists,
    grid_latent,
    grid_edges,
    grid_sender,
    proc_edge_in,
    proc_edge_out,
    proc_node_in,
    proc_node_out,
    grid_edge_in,
    grid_edge_out,
    grid_node_in,
    grid_node_out,
    proc_edge_gain,
    proc_node_gain,
    grid_edge_gain,
    grid_node_gain,
):
    n = lax.axis_size("lon")
    rows, width = mesh_latent.shape
    cap = proc_lists.shape[1]
    n_tab = n * cap
    n_edges = mesh_edges.shape[0]
    n_gedges = grid_edges.shape[0]
    n_grid = grid_latent.shape[0]
    big = (
        mesh_edges,
        grid_latent,
        grid_edges,
        proc_edge_in,
        proc_edge_out,
        proc_node_in,
        proc_node_out,
        grid_edge_in,
        grid_edge_out,
        grid_node_in,
        grid_node_out,
    )
    small = (
        mesh_latent,
        proc_lists.T,
        proc_slot,
        proc_receiver,
        grid_sender,
        proc_edge_gain.reshape(1, -1),
        proc_node_gain.reshape(1, -1),
        grid_edge_gain.reshape(1, -1),
        grid_node_gain.reshape(1, -1),
    )
    vmem = pl.BlockSpec(memory_space=pltpu.VMEM)
    return pl.pallas_call(
        functools.partial(kernel, n),
        out_shape=(
            jax.ShapeDtypeStruct(mesh_latent.shape, BF16),
            jax.ShapeDtypeStruct(grid_latent.shape, BF16),
        ),
        in_specs=[pl.BlockSpec(memory_space=pltpu.HBM)] * len(big + small),
        out_specs=(vmem, vmem),
        scratch_shapes=[pltpu.VMEM(a.shape, a.dtype) for a in big + small]
        + [
            pltpu.VMEM((1, n_edges), jnp.int32),
            pltpu.VMEM((1, n_edges), jnp.int32),
            pltpu.VMEM((1, n_gedges), jnp.int32),
            pltpu.VMEM((n, cap, LANES), jnp.int32),
            pltpu.VMEM((n, cap, LANES), jnp.int32),
            pltpu.VMEM((n_tab * 2, width // 2), BF16),
            pltpu.VMEM((n_tab * 2, width // 2), BF16),
            pltpu.VMEM((LANES, width), BF16),
            pltpu.VMEM((n_tab + LANES, width), BF16),
            pltpu.VMEM((n_edges, width), F32),
            pltpu.VMEM((n_gedges, width), F32),
            pltpu.VMEM((n_grid, width), F32),
            pltpu.VMEM((rows, width), F32),
            pltpu.VMEM((rows, width), BF16),
            pltpu.VMEM((2 * rows, width), BF16),
            pltpu.VMEM((n_grid, width), BF16),
            pltpu.SemaphoreType.DMA((len(big + small),)),
            pltpu.SemaphoreType.DMA,
            pltpu.SemaphoreType.DMA,
            pltpu.SemaphoreType.DMA,
            pltpu.SemaphoreType.DMA,
            pltpu.SemaphoreType.DMA((2,)),
            pltpu.SemaphoreType.DMA((2,)),
        ],
        compiler_params=pltpu.CompilerParams(
            collective_id=0, has_side_effects=True, vmem_limit_bytes=62 * 1024 * 1024
        ),
    )(*big, *small)


def solution(mesh):
    rows = P(("groups", "lon"), None)
    flat = P(("groups", "lon"))
    placed = (rows, rows, flat, flat, rows, rows, rows, flat) + (P(),) * 12
    return jax.shard_map(
        local,
        mesh=mesh,
        in_specs=placed,
        out_specs=(rows, rows),
        check_vma=False,
    )
```

```python
import functools

import jax
import jax.numpy as jnp
from jax import lax
from jax.experimental import pallas as pl
from jax.experimental.pallas import tpu as pltpu
from jax.sharding import PartitionSpec as P

NEAR = 3
EPSILON = 1e-05
BLOCK = 384
LANES = 128
BF16 = jnp.bfloat16
F32 = jnp.float32
MESH_ID = pl.DeviceIdType.MESH


def mm(a, b):
    return jnp.dot(a, b, preferred_element_type=F32)


def mm_t(a, b):
    return lax.dot_general(a, b, (((0,), (0,)), ((), ())), preferred_element_type=F32)


def pick(flags):
    return jnp.where(flags, 1.0, 0.0).astype(BF16)


def act(first_sum):
    half = 0.5 * first_sum
    return (half + half * jnp.tanh(half)).astype(BF16)


def norm(values, gain):
    center = values - jnp.mean(values, axis=-1, keepdims=True)
    spread = jnp.mean(center * center, axis=-1, keepdims=True)
    return center * lax.rsqrt(spread + EPSILON) * gain


def iota(shape, dim):
    return lax.broadcasted_iota(jnp.int32, shape, dim)


def kernel(
    n,
    *refs,
):
    hbm = refs[:20]
    mesh_out, grid_out = refs[20:22]
    vm = refs[22:42]
    (
        slot,
        recv,
        gsend,
        list_src,
        list_dst,
        rows_src,
        rows_dst,
        term_pad,
        table,
        edge_acc,
        grid_acc,
        gnode_acc,
        incoming,
        own_term,
        side_term,
        gin,
        load_sem,
        list_send,
        list_recv,
        rows_send,
        rows_recv,
        side_send,
        side_recv,
    ) = refs[42:]
    edges, glat, gedges, pe_in, pe_out, pn_in, pn_out, ge_in, ge_out, gn_in, gn_out = vm[:11]
    lat, lists, slot_flat, recv_flat, gsend_flat, pe_gain, pn_gain, ge_gain, gn_gain = vm[11:]
    order = (12, 11, 3, 0, 13, 14, 5, 7, 2, 1, 9, 4, 6, 15, 16, 17, 18, 19, 8, 10)

    def load(k):
        return pltpu.make_async_copy(hbm[k], vm[k], load_sem.at[k])

    for k in order:
        load(k).start()

    me = lax.axis_index("lon")
    rows, width = lat.shape
    cap = lists.shape[0]
    half = width // 2
    n_tab = n * cap
    n_edges = edges.shape[0]
    n_gedges = gedges.shape[0]
    n_grid = glat.shape[0]
    nodes = BLOCK // NEAR

    def at(distance):
        return lax.rem(me + distance + n, n)

    barrier = pltpu.get_barrier_semaphore()

    def greet(d, carry):
        pl.semaphore_signal(barrier, inc=1, device_id={"lon": at(d)}, device_id_type=MESH_ID)
        return carry

    lax.fori_loop(1, n, greet, 0)

    def spread_list(o, carry):
        kept = jnp.where(iota((cap, n), 1) == o, lists[...].astype(F32), 0.0)
        column = jnp.sum(kept, axis=1, keepdims=True)
        list_src[o] = jnp.broadcast_to(column, (cap, LANES)).astype(jnp.int32)
        return carry

    load(12).wait()
    lax.fori_loop(0, n, spread_list, 0)
    pl.semaphore_wait(barrier, n - 1)

    def list_copy(d):
        return pltpu.make_async_remote_copy(
            src_ref=list_src.at[at(d)],
            dst_ref=list_dst.at[d],
            send_sem=list_send,
            recv_sem=list_recv,
            device_id={"lon": at(d)},
            device_id_type=MESH_ID,
        )

    def send_list(d, carry):
        list_copy(d).start()
        return carry

    lax.fori_loop(1, n, send_list, 0)
    list_dst[0] = list_src[me]

    load(11).wait()
    load(3).wait()
    lat_v = lat[...]
    term_pad[...] = jnp.zeros_like(term_pad)
    term_pad[0:rows, :] = mm(lat_v, pe_in[width : 2 * width, :]).astype(BF16)
    table[n_tab:, :] = jnp.zeros((LANES, width), BF16)
    table[n_tab : n_tab + rows, :] = mm(lat_v, pe_in[2 * width :, :]).astype(BF16)

    load(0).wait()

    def edge_first(b, carry):
        here = pl.ds(pl.multiple_of(b * BLOCK, BLOCK), BLOCK)
        edge_acc[here, :] = mm(edges[here, :], pe_in[0:width, :])
        return carry

    lax.fori_loop(0, n_edges // BLOCK, edge_first, 0, unroll=True)

    got = list_dst.at[pl.ds(1, n - 1)]
    pltpu.make_async_copy(got, got, list_recv).wait()
    wanted = list_dst[...].reshape(n_tab, LANES)
    chosen = pick(wanted == iota((n_tab, LANES), 1))
    left_half = mm(chosen, term_pad[:, 0:half]).reshape(n, cap, half)
    right_half = mm(chosen, term_pad[:, half:]).reshape(n, cap, half)
    rows_src[...] = (
        jnp.concatenate([left_half, right_half], axis=1).reshape(n_tab * 2, half).astype(BF16)
    )
    chunk = 2 * cap

    def rows_copy(d):
        return pltpu.make_async_remote_copy(
            src_ref=rows_src.at[pl.ds(pl.multiple_of(d * chunk, chunk), chunk), :],
            dst_ref=rows_dst.at[pl.ds(pl.multiple_of((n - d) * chunk, chunk), chunk), :],
            send_sem=rows_send,
            recv_sem=rows_recv,
            device_id={"lon": at(-d)},
            device_id_type=MESH_ID,
        )

    def send_rows(d, carry):
        rows_copy(d).start()
        return carry

    lax.fori_loop(1, n, send_rows, 0)
    rows_dst[0:chunk, :] = rows_src[0:chunk, :]

    for k in (13, 14, 5, 7):
        load(k).wait()
    slot[...] = slot_flat[...].reshape(1, n_edges)
    recv[...] = recv_flat[...].reshape(1, n_edges)
    load(2).wait()
    load(1).wait()
    node_own = mm(lat_v, pn_in[0:width, :])
    repeat = pick(iota((BLOCK, nodes), 0) // NEAR == iota((BLOCK, nodes), 1))

    def grid_first(b, carry):
        here = pl.ds(pl.multiple_of(b * BLOCK, BLOCK), BLOCK)
        there = pl.ds(pl.multiple_of(b * nodes, nodes), nodes)
        term = mm(glat[there, :], ge_in[2 * width :, :]).astype(BF16)
        grid_acc[here, :] = mm(gedges[here, :], ge_in[0:width, :]) + mm(repeat, term)
        return carry

    lax.fori_loop(0, n_gedges // BLOCK, grid_first, 0, unroll=True)
    load(9).wait()
    gnode_acc[...] = mm(glat[...], gn_in[0:width, :])
    for k in (4, 6, 15, 16, 17, 18, 19):
        load(k).wait()
    gsend[...] = gsend_flat[...].reshape(1, n_gedges)

    arrived = rows_dst.at[pl.ds(chunk, (n - 1) * chunk), :]
    pltpu.make_async_copy(arrived, arrived, rows_recv).wait()
    parts = rows_dst[...].astype(F32).reshape(n, 2, cap, half)
    table[0:n_tab, :] = jnp.concatenate(
        [parts[:, 0].reshape(n_tab, half), parts[:, 1].reshape(n_tab, half)], axis=1
    ).astype(BF16)

    distance = me - iota((n, cap, BLOCK), 0)
    owner = jnp.where(distance < 0, distance + n, distance)
    slot_of = (owner * cap + iota((n, cap, BLOCK), 1)).reshape(n_tab, BLOCK)
    incoming[...] = jnp.zeros_like(incoming)

    def edge_second(b, carry):
        here = pl.ds(pl.multiple_of(b * BLOCK, BLOCK), BLOCK)
        slots = slot[:, here]
        receivers = recv[:, here]
        gather = jnp.concatenate(
            [
                pick(slot_of == slots),
                pick(iota((LANES, BLOCK), 0) == jnp.minimum(receivers, rows - 1)),
            ],
            axis=0,
        )
        total = edge_acc[here, :] + mm_t(gather, table[...])
        message = norm(mm(act(total), pe_out[...]), pe_gain[...]).astype(BF16)
        incoming[...] += mm(pick(iota((rows, BLOCK), 0) == receivers), message)
        return carry

    lax.fori_loop(0, n_edges // BLOCK, edge_second, 0, unroll=True)

    node_sum = node_own + mm(incoming[...].astype(BF16), pn_in[width:, :])
    mesh_new = (
        lat_v.astype(F32) + norm(mm(act(node_sum), pn_out[...]), pn_gain[...])
    ).astype(BF16)
    mesh_out[...] = mesh_new
    own_term[...] = mm(mesh_new, ge_in[width : 2 * width, :]).astype(BF16)

    def side_copy(side):
        return pltpu.make_async_remote_copy(
            src_ref=own_term,
            dst_ref=side_term.at[pl.ds(side * rows, rows), :],
            send_sem=side_send.at[side],
            recv_sem=side_recv.at[side],
            device_id={"lon": at(1 - 2 * side)},
            device_id_type=MESH_ID,
        )

    side_copy(0).start()
    side_copy(1).start()
    load(8).wait()
    load(10).wait()

    def grid_own(b, carry):
        here = pl.ds(pl.multiple_of(b * BLOCK, BLOCK), BLOCK)
        gather = pick(iota((rows, BLOCK), 0) + me * rows == gsend[:, here])
        grid_acc[here, :] += mm_t(gather, own_term[...])
        return carry

    lax.fori_loop(0, n_gedges // BLOCK, grid_own, 0, unroll=True)
    side_copy(0).wait_recv()
    side_copy(1).wait_recv()
    pooled = pick(iota((nodes, BLOCK), 1) // NEAR == iota((nodes, BLOCK), 0))
    side_index = jnp.concatenate(
        [iota((rows, BLOCK), 0) + at(-1) * rows, iota((rows, BLOCK), 0) + at(1) * rows], axis=0
    )

    def grid_second(b, carry):
        here = pl.ds(pl.multiple_of(b * BLOCK, BLOCK), BLOCK)
        there = pl.ds(pl.multiple_of(b * nodes, nodes), nodes)
        gather = pick(side_index == gsend[:, here])
        total = grid_acc[here, :] + mm_t(gather, side_term[...])
        message = norm(mm(act(total), ge_out[...]), ge_gain[...]).astype(BF16)
        gin[there, :] = mm(pooled, message).astype(BF16)
        return carry

    lax.fori_loop(0, n_gedges // BLOCK, grid_second, 0, unroll=True)

    def grid_node(b, carry):
        there = pl.ds(pl.multiple_of(b * (n_grid // 2), n_grid // 2), n_grid // 2)
        total = gnode_acc[there, :] + mm(gin[there, :], gn_in[width:, :])
        update = norm(mm(act(total), gn_out[...]), gn_gain[...])
        grid_out[there, :] = (glat[there, :].astype(F32) + update).astype(BF16)
        return carry

    lax.fori_loop(0, 2, grid_node, 0, unroll=True)

    sent = list_src.at[pl.ds(1, n - 1)]
    pltpu.make_async_copy(sent, sent, list_send).wait()
    gone = rows_src.at[pl.ds(chunk, (n - 1) * chunk), :]
    pltpu.make_async_copy(gone, gone, rows_send).wait()
    side_copy(0).wait_send()
    side_copy(1).wait_send()


def local(
    mesh_latent,
    mesh_edges,
    proc_slot,
    proc_receiver,
    proc_lists,
    grid_latent,
    grid_edges,
    grid_sender,
    proc_edge_in,
    proc_edge_out,
    proc_node_in,
    proc_node_out,
    grid_edge_in,
    grid_edge_out,
    grid_node_in,
    grid_node_out,
    proc_edge_gain,
    proc_node_gain,
    grid_edge_gain,
    grid_node_gain,
):
    n = lax.axis_size("lon")
    rows, width = mesh_latent.shape
    cap = proc_lists.shape[1]
    n_tab = n * cap
    n_edges = mesh_edges.shape[0]
    n_gedges = grid_edges.shape[0]
    n_grid = grid_latent.shape[0]
    big = (
        mesh_edges,
        grid_latent,
        grid_edges,
        proc_edge_in,
        proc_edge_out,
        proc_node_in,
        proc_node_out,
        grid_edge_in,
        grid_edge_out,
        grid_node_in,
        grid_node_out,
    )
    small = (
        mesh_latent,
        proc_lists.T,
        proc_slot,
        proc_receiver,
        grid_sender,
        proc_edge_gain.reshape(1, -1),
        proc_node_gain.reshape(1, -1),
        grid_edge_gain.reshape(1, -1),
        grid_node_gain.reshape(1, -1),
    )
    vmem = pl.BlockSpec(memory_space=pltpu.VMEM)
    return pl.pallas_call(
        functools.partial(kernel, n),
        out_shape=(
            pltpu.VMEM(mesh_latent.shape, BF16),
            pltpu.VMEM(grid_latent.shape, BF16),
        ),
        in_specs=[pl.BlockSpec(memory_space=pltpu.HBM)] * len(big + small),
        out_specs=(vmem, vmem),
        scratch_shapes=[pltpu.VMEM(a.shape, a.dtype) for a in big + small]
        + [
            pltpu.VMEM((1, n_edges), jnp.int32),
            pltpu.VMEM((1, n_edges), jnp.int32),
            pltpu.VMEM((1, n_gedges), jnp.int32),
            pltpu.VMEM((n, cap, LANES), jnp.int32),
            pltpu.VMEM((n, cap, LANES), jnp.int32),
            pltpu.VMEM((n_tab * 2, width // 2), BF16),
            pltpu.VMEM((n_tab * 2, width // 2), BF16),
            pltpu.VMEM((LANES, width), BF16),
            pltpu.VMEM((n_tab + LANES, width), BF16),
            pltpu.VMEM((n_edges, width), F32),
            pltpu.VMEM((n_gedges, width), F32),
            pltpu.VMEM((n_grid, width), F32),
            pltpu.VMEM((rows, width), F32),
            pltpu.VMEM((rows, width), BF16),
            pltpu.VMEM((2 * rows, width), BF16),
            pltpu.VMEM((n_grid, width), BF16),
            pltpu.SemaphoreType.DMA((len(big + small),)),
            pltpu.SemaphoreType.DMA,
            pltpu.SemaphoreType.DMA,
            pltpu.SemaphoreType.DMA,
            pltpu.SemaphoreType.DMA,
            pltpu.SemaphoreType.DMA((2,)),
            pltpu.SemaphoreType.DMA((2,)),
        ],
        compiler_params=pltpu.CompilerParams(
            collective_id=0, has_side_effects=True, vmem_limit_bytes=62 * 1024 * 1024
        ),
    )(*big, *small)


def solution(mesh):
    rows = P(("groups", "lon"), None)
    flat = P(("groups", "lon"))
    placed = (rows, rows, flat, flat, rows, rows, rows, flat) + (P(),) * 12
    return jax.shard_map(
        local,
        mesh=mesh,
        in_specs=placed,
        out_specs=(rows, rows),
        check_vma=False,
    )
```

```python
import functools

import jax
import jax.numpy as jnp
from jax import lax
from jax.experimental import pallas as pl
from jax.experimental.pallas import tpu as pltpu
from jax.sharding import PartitionSpec as P

NEAR = 3
EPSILON = 1e-05
BLOCK = 384
LANES = 128
BF16 = jnp.bfloat16
F32 = jnp.float32
MESH_ID = pl.DeviceIdType.MESH


def mm(a, b):
    return jnp.dot(a, b, preferred_element_type=F32)


def mm_t(a, b):
    return lax.dot_general(a, b, (((0,), (0,)), ((), ())), preferred_element_type=F32)


def pick(flags):
    return jnp.where(flags, 1.0, 0.0).astype(BF16)


def act(first_sum):
    half = 0.5 * first_sum
    return (half + half * jnp.tanh(half)).astype(BF16)


def norm(values, gain):
    center = values - jnp.mean(values, axis=-1, keepdims=True)
    spread = jnp.mean(center * center, axis=-1, keepdims=True)
    return center * lax.rsqrt(spread + EPSILON) * gain


def iota(shape, dim):
    return lax.broadcasted_iota(jnp.int32, shape, dim)


def kernel(
    n,
    *refs,
):
    hbm = refs[:20]
    mesh_out, grid_out = refs[20:22]
    vm = refs[22:42]
    (
        slot,
        recv,
        gsend,
        list_src,
        list_dst,
        rows_src,
        rows_dst,
        term_pad,
        table,
        edge_acc,
        grid_acc,
        gnode_acc,
        incoming,
        own_term,
        side_term,
        gin,
        load_sem,
        list_send,
        list_recv,
        rows_send,
        rows_recv,
        side_send,
        side_recv,
    ) = refs[42:]
    edges, glat, gedges, pe_in, pe_out, pn_in, pn_out, ge_in, ge_out, gn_in, gn_out = vm[:11]
    lat, lists, slot_flat, recv_flat, gsend_flat, pe_gain, pn_gain, ge_gain, gn_gain = vm[11:]
    order = (12, 11, 3, 0, 13, 14, 5, 7, 2, 1, 9, 4, 6, 15, 16, 17, 18, 19, 8, 10)

    def load(k):
        return pltpu.make_async_copy(hbm[k], vm[k], load_sem.at[k])

    for k in order:
        load(k).start()

    me = lax.axis_index("lon")
    rows, width = lat.shape
    cap = lists.shape[0]
    half = width // 2
    n_tab = n * cap
    n_edges = edges.shape[0]
    n_gedges = gedges.shape[0]
    n_grid = glat.shape[0]
    nodes = BLOCK // NEAR

    def at(distance):
        return lax.rem(me + distance + n, n)

    barrier = pltpu.get_barrier_semaphore()

    def greet(d, carry):
        pl.semaphore_signal(barrier, inc=1, device_id={"lon": at(d)}, device_id_type=MESH_ID)
        return carry

    lax.fori_loop(1, n, greet, 0, unroll=n <= 16)

    def spread_list(o, carry):
        kept = jnp.where(iota((cap, n), 1) == o, lists[...].astype(F32), 0.0)
        column = jnp.sum(kept, axis=1, keepdims=True)
        list_src[o] = jnp.broadcast_to(column, (cap, LANES)).astype(jnp.int32)
        return carry

    load(12).wait()
    lax.fori_loop(0, n, spread_list, 0)
    pl.semaphore_wait(barrier, n - 1)

    def list_copy(d):
        return pltpu.make_async_remote_copy(
            src_ref=list_src.at[at(d)],
            dst_ref=list_dst.at[d],
            send_sem=list_send,
            recv_sem=list_recv,
            device_id={"lon": at(d)},
            device_id_type=MESH_ID,
        )

    def send_list(d, carry):
        list_copy(d).start()
        return carry

    lax.fori_loop(1, n, send_list, 0, unroll=n <= 16)
    list_dst[0] = list_src[me]

    load(11).wait()
    load(3).wait()
    lat_v = lat[...]
    term_pad[...] = jnp.zeros_like(term_pad)
    term_pad[0:rows, :] = mm(lat_v, pe_in[width : 2 * width, :]).astype(BF16)
    table[n_tab:, :] = jnp.zeros((LANES, width), BF16)
    table[n_tab : n_tab + rows, :] = mm(lat_v, pe_in[2 * width :, :]).astype(BF16)

    load(0).wait()

    def edge_first(b, carry):
        here = pl.ds(pl.multiple_of(b * BLOCK, BLOCK), BLOCK)
        edge_acc[here, :] = mm(edges[here, :], pe_in[0:width, :])
        return carry

    lax.fori_loop(0, n_edges // BLOCK, edge_first, 0, unroll=True)

    got = list_dst.at[pl.ds(1, n - 1)]
    pltpu.make_async_copy(got, got, list_recv).wait()
    wanted = list_dst[...].reshape(n_tab, LANES)
    chosen = pick(wanted == iota((n_tab, LANES), 1))
    left_half = mm(chosen, term_pad[:, 0:half]).reshape(n, cap, half)
    right_half = mm(chosen, term_pad[:, half:]).reshape(n, cap, half)
    rows_src[...] = (
        jnp.concatenate([left_half, right_half], axis=1).reshape(n_tab * 2, half).astype(BF16)
    )
    chunk = 2 * cap

    def rows_copy(d):
        return pltpu.make_async_remote_copy(
            src_ref=rows_src.at[pl.ds(pl.multiple_of(d * chunk, chunk), chunk), :],
            dst_ref=rows_dst.at[pl.ds(pl.multiple_of((n - d) * chunk, chunk), chunk), :],
            send_sem=rows_send,
            recv_sem=rows_recv,
            device_id={"lon": at(-d)},
            device_id_type=MESH_ID,
        )

    def send_rows(d, carry):
        rows_copy(d).start()
        return carry

    lax.fori_loop(1, n, send_rows, 0, unroll=n <= 16)
    rows_dst[0:chunk, :] = rows_src[0:chunk, :]

    for k in (13, 14, 5, 7):
        load(k).wait()
    slot[...] = slot_flat[...].reshape(1, n_edges)
    recv[...] = recv_flat[...].reshape(1, n_edges)
    load(2).wait()
    load(1).wait()
    node_own = mm(lat_v, pn_in[0:width, :])
    repeat = pick(iota((BLOCK, nodes), 0) // NEAR == iota((BLOCK, nodes), 1))

    def grid_first(b, carry):
        here = pl.ds(pl.multiple_of(b * BLOCK, BLOCK), BLOCK)
        there = pl.ds(pl.multiple_of(b * nodes, nodes), nodes)
        term = mm(glat[there, :], ge_in[2 * width :, :]).astype(BF16)
        grid_acc[here, :] = mm(gedges[here, :], ge_in[0:width, :]) + mm(repeat, term)
        return carry

    lax.fori_loop(0, n_gedges // BLOCK, grid_first, 0, unroll=True)
    load(9).wait()
    gnode_acc[...] = mm(glat[...], gn_in[0:width, :])
    for k in (4, 6, 15, 16, 17, 18, 19):
        load(k).wait()
    gsend[...] = gsend_flat[...].reshape(1, n_gedges)

    arrived = rows_dst.at[pl.ds(chunk, (n - 1) * chunk), :]
    pltpu.make_async_copy(arrived, arrived, rows_recv).wait()
    parts = rows_dst[...].astype(F32).reshape(n, 2, cap, half)
    table[0:n_tab, :] = jnp.concatenate(
        [parts[:, 0].reshape(n_tab, half), parts[:, 1].reshape(n_tab, half)], axis=1
    ).astype(BF16)

    distance = me - iota((n, cap, BLOCK), 0)
    owner = jnp.where(distance < 0, distance + n, distance)
    slot_of = (owner * cap + iota((n, cap, BLOCK), 1)).reshape(n_tab, BLOCK)
    incoming[...] = jnp.zeros_like(incoming)

    def edge_second(b, carry):
        here = pl.ds(pl.multiple_of(b * BLOCK, BLOCK), BLOCK)
        slots = slot[:, here]
        receivers = recv[:, here]
        gather = jnp.concatenate(
            [
                pick(slot_of == slots),
                pick(iota((LANES, BLOCK), 0) == jnp.minimum(receivers, rows - 1)),
            ],
            axis=0,
        )
        total = edge_acc[here, :] + mm_t(gather, table[...])
        message = norm(mm(act(total), pe_out[...]), pe_gain[...]).astype(BF16)
        incoming[...] += mm(pick(iota((rows, BLOCK), 0) == receivers), message)
        return carry

    lax.fori_loop(0, n_edges // BLOCK, edge_second, 0, unroll=True)

    node_sum = node_own + mm(incoming[...].astype(BF16), pn_in[width:, :])
    mesh_new = (
        lat_v.astype(F32) + norm(mm(act(node_sum), pn_out[...]), pn_gain[...])
    ).astype(BF16)
    mesh_out[...] = mesh_new
    own_term[...] = mm(mesh_new, ge_in[width : 2 * width, :]).astype(BF16)

    def side_copy(side):
        return pltpu.make_async_remote_copy(
            src_ref=own_term,
            dst_ref=side_term.at[pl.ds(side * rows, rows), :],
            send_sem=side_send.at[side],
            recv_sem=side_recv.at[side],
            device_id={"lon": at(1 - 2 * side)},
            device_id_type=MESH_ID,
        )

    side_copy(0).start()
    side_copy(1).start()
    load(8).wait()
    load(10).wait()

    def grid_own(b, carry):
        here = pl.ds(pl.multiple_of(b * BLOCK, BLOCK), BLOCK)
        gather = pick(iota((rows, BLOCK), 0) + me * rows == gsend[:, here])
        grid_acc[here, :] += mm_t(gather, own_term[...])
        return carry

    lax.fori_loop(0, n_gedges // BLOCK, grid_own, 0, unroll=True)
    side_copy(0).wait_recv()
    side_copy(1).wait_recv()
    pooled = pick(iota((nodes, BLOCK), 1) // NEAR == iota((nodes, BLOCK), 0))
    side_index = jnp.concatenate(
        [iota((rows, BLOCK), 0) + at(-1) * rows, iota((rows, BLOCK), 0) + at(1) * rows], axis=0
    )

    def grid_second(b, carry):
        here = pl.ds(pl.multiple_of(b * BLOCK, BLOCK), BLOCK)
        there = pl.ds(pl.multiple_of(b * nodes, nodes), nodes)
        gather = pick(side_index == gsend[:, here])
        total = grid_acc[here, :] + mm_t(gather, side_term[...])
        message = norm(mm(act(total), ge_out[...]), ge_gain[...]).astype(BF16)
        gin[there, :] = mm(pooled, message).astype(BF16)
        return carry

    lax.fori_loop(0, n_gedges // BLOCK, grid_second, 0, unroll=True)

    def grid_node(b, carry):
        there = pl.ds(pl.multiple_of(b * (n_grid // 2), n_grid // 2), n_grid // 2)
        total = gnode_acc[there, :] + mm(gin[there, :], gn_in[width:, :])
        update = norm(mm(act(total), gn_out[...]), gn_gain[...])
        grid_out[there, :] = (glat[there, :].astype(F32) + update).astype(BF16)
        return carry

    lax.fori_loop(0, 2, grid_node, 0, unroll=True)

    sent = list_src.at[pl.ds(1, n - 1)]
    pltpu.make_async_copy(sent, sent, list_send).wait()
    gone = rows_src.at[pl.ds(chunk, (n - 1) * chunk), :]
    pltpu.make_async_copy(gone, gone, rows_send).wait()
    side_copy(0).wait_send()
    side_copy(1).wait_send()


def local(
    mesh_latent,
    mesh_edges,
    proc_slot,
    proc_receiver,
    proc_lists,
    grid_latent,
    grid_edges,
    grid_sender,
    proc_edge_in,
    proc_edge_out,
    proc_node_in,
    proc_node_out,
    grid_edge_in,
    grid_edge_out,
    grid_node_in,
    grid_node_out,
    proc_edge_gain,
    proc_node_gain,
    grid_edge_gain,
    grid_node_gain,
):
    n = lax.axis_size("lon")
    rows, width = mesh_latent.shape
    cap = proc_lists.shape[1]
    n_tab = n * cap
    n_edges = mesh_edges.shape[0]
    n_gedges = grid_edges.shape[0]
    n_grid = grid_latent.shape[0]
    big = (
        mesh_edges,
        grid_latent,
        grid_edges,
        proc_edge_in,
        proc_edge_out,
        proc_node_in,
        proc_node_out,
        grid_edge_in,
        grid_edge_out,
        grid_node_in,
        grid_node_out,
    )
    small = (
        mesh_latent,
        proc_lists.T,
        proc_slot,
        proc_receiver,
        grid_sender,
        proc_edge_gain.reshape(1, -1),
        proc_node_gain.reshape(1, -1),
        grid_edge_gain.reshape(1, -1),
        grid_node_gain.reshape(1, -1),
    )
    vmem = pl.BlockSpec(memory_space=pltpu.VMEM)
    return pl.pallas_call(
        functools.partial(kernel, n),
        out_shape=(
            pltpu.VMEM(mesh_latent.shape, BF16),
            pltpu.VMEM(grid_latent.shape, BF16),
        ),
        in_specs=[pl.BlockSpec(memory_space=pltpu.HBM)] * len(big + small),
        out_specs=(vmem, vmem),
        scratch_shapes=[pltpu.VMEM(a.shape, a.dtype) for a in big + small]
        + [
            pltpu.VMEM((1, n_edges), jnp.int32),
            pltpu.VMEM((1, n_edges), jnp.int32),
            pltpu.VMEM((1, n_gedges), jnp.int32),
            pltpu.VMEM((n, cap, LANES), jnp.int32),
            pltpu.VMEM((n, cap, LANES), jnp.int32),
            pltpu.VMEM((n_tab * 2, width // 2), BF16),
            pltpu.VMEM((n_tab * 2, width // 2), BF16),
            pltpu.VMEM((LANES, width), BF16),
            pltpu.VMEM((n_tab + LANES, width), BF16),
            pltpu.VMEM((n_edges, width), F32),
            pltpu.VMEM((n_gedges, width), F32),
            pltpu.VMEM((n_grid, width), F32),
            pltpu.VMEM((rows, width), F32),
            pltpu.VMEM((rows, width), BF16),
            pltpu.VMEM((2 * rows, width), BF16),
            pltpu.VMEM((n_grid, width), BF16),
            pltpu.SemaphoreType.DMA((len(big + small),)),
            pltpu.SemaphoreType.DMA,
            pltpu.SemaphoreType.DMA,
            pltpu.SemaphoreType.DMA,
            pltpu.SemaphoreType.DMA,
            pltpu.SemaphoreType.DMA((2,)),
            pltpu.SemaphoreType.DMA((2,)),
        ],
        compiler_params=pltpu.CompilerParams(
            collective_id=0, has_side_effects=True, vmem_limit_bytes=62 * 1024 * 1024
        ),
    )(*big, *small)


def solution(mesh):
    rows = P(("groups", "lon"), None)
    flat = P(("groups", "lon"))
    placed = (rows, rows, flat, flat, rows, rows, rows, flat) + (P(),) * 12
    return jax.shard_map(
        local,
        mesh=mesh,
        in_specs=placed,
        out_specs=(rows, rows),
        check_vma=False,
    )
```
